32 devices in a mesh: va: 4 (over y, x), vb: 4 (over z), pair: 2 (over core).
Axes of the slice: x: 2, y: 2, z: 4, core: 2. Of those that a mesh axis runs over, the one named last changes fastest.
Arguments:
- left_fit: bfloat16 [30, 2048, 1536], P('pair', 'va'), may hold values from -0.5 to 0.5
- right_fit: bfloat16 [30, 2048, 1536], P('pair', 'vb'), may hold values from -0.5 to 0.5
- occ_energy: float32 [8], replicated, may hold values from -1.5 to -0.3
- virt_energy: float32 [2048], replicated, may hold values from 0.2 to 2
- pair_list: int32 [30, 2], P('pair'), may hold values from 0 to 7, as said below
- domain_blocks: int32 [30, 12], P('pair'), may hold values from 0 to 31, as said below
Outputs:
- density: float32 [4096, 8, 2048], P(('vb', 'pair'), None, 'va')
The draws below stay inside these ranges and needn't reach their ends.
Inputs may be any that keep to these rules, and one draw needn't show every extreme that they name: `domain_blocks`: the 12 entries of a row are distinct. `pair_list`: each row holds two orbitals i <= j, and no two rows are the same pair.
All inputs are finite; a program needn't handle non-finite values.
Results may differ from the reference program's by a relative error of at most 0.0028.
Values may be sent and summed in bfloat16 or wider, within the bound.
A program may use at most 256 MiB of HBM per device.

```python
import jax
import jax.numpy as jnp
from jax import lax

V = 2048
BLOCK = 128
DOM_BLK = 12
NOCC = 8
AUX_BLK = 32
DOM = 1536
PAIRS = 30


def draw_domain_blocks(key, part):
    row_keys = jax.random.split(key, PAIRS)

    def pick_row(row_key):
        return jax.random.permutation(row_key, AUX_BLK)[:DOM_BLK]
    chosen = jax.vmap(pick_row)(row_keys)
    return chosen.astype(jnp.int32)


def draw_pair_list(key, part):
    square = NOCC * NOCC
    flat_cells = jnp.arange(square, dtype=jnp.int32)
    first_orb = flat_cells // NOCC
    second_orb = flat_cells % NOCC
    rank_keys = jax.random.permutation(jax.random.fold_in(key, 17), square).astype(jnp.int32)
    rank_keys = jnp.where(first_orb <= second_orb, rank_keys, rank_keys + square)
    rank_keys = jnp.where((first_orb == 0) & (second_orb == NOCC - 1), -1, rank_keys)
    picked = jnp.argsort(rank_keys, stable=True)[:PAIRS]
    return jnp.stack([first_orb[picked], second_orb[picked]], axis=1).astype(jnp.int32)


def steps_of(rng, shape, cuts, least, largest):
    def one(axis_at, blocks):
        draws = jax.random.uniform(jax.random.fold_in(jax.random.fold_in(rng, 6), axis_at), (blocks,), jnp.float32, least / len(cuts), largest / len(cuts))
        return jnp.repeat(jnp.exp(draws), shape[axis_at] // blocks).reshape((-1,) + (1,) * (len(shape) - axis_at - 1))

    loudness = one(*cuts[0])
    for cut in cuts[1:]:
        loudness = loudness * one(*cut)
    return loudness


def centred(rng, extent, scale, bound, cuts=(), kind=jnp.bfloat16):
    entries = scale * jax.random.normal(rng, extent, jnp.float32)
    if cuts:
        entries = entries * steps_of(rng, extent, cuts, -0.22, 0.18)
    return jnp.clip(entries, -bound, bound).astype(kind)


def setup_inputs(seed: int = 0) -> dict:
    key_list = jax.random.split(jax.random.key(seed), 7)
    return {
        "left_fit": centred(key_list[0], (PAIRS, V, DOM), 0.08, 0.5, ((0, 2), (1, 4))),
        "right_fit": centred(key_list[1], (PAIRS, V, DOM), 0.08, 0.5, ((0, 2), (1, 4))),
        "occ_energy": jnp.clip(jax.random.uniform(key_list[2], (NOCC,), jnp.float32, -1.5, -0.3), -1.5, -0.3),
        "virt_energy": jnp.clip(jax.random.uniform(key_list[3], (V,), jnp.float32, 0.2, 2.0), 0.2, 2.0),
        "pair_list": draw_pair_list(jax.random.fold_in(key_list[6], 71), 0),
        "domain_blocks": draw_domain_blocks(jax.random.fold_in(key_list[6], 71), 0),
    }


def reference(left_fit, right_fit, occ_energy, virt_energy, pair_list, domain_blocks):
    total_pairs = left_fit.shape[0]

    def one_pair(running, pair_index):
        left_rows = left_fit[pair_index]
        right_rows = right_fit[pair_index]
        coulomb = jnp.dot(left_rows, right_rows.T, preferred_element_type=jnp.float32).astype(jnp.bfloat16)
        first_occ = pair_list[pair_index, 0]
        second = pair_list[pair_index, 1]
        energy_gap = virt_energy[:, None] + virt_energy[None, :] - occ_energy[first_occ] - occ_energy[second]
        coulomb_wide = coulomb.astype(jnp.float32)
        amplitude = ((2.0 * coulomb_wide - coulomb_wide.T) / energy_gap).astype(jnp.bfloat16)
        contracted = jnp.dot(right_rows.T, amplitude.T, preferred_element_type=jnp.float32)
        pieces = contracted.reshape(DOM_BLK, BLOCK, V)
        running = running.at[domain_blocks[pair_index], first_occ].add(pieces)
        return running, None

    zero_dense = jnp.zeros((AUX_BLK, NOCC, BLOCK, V), jnp.float32)
    accumulated, unused = lax.scan(one_pair, zero_dense, jnp.arange(total_pairs, dtype=jnp.int32))
    return accumulated.transpose(0, 2, 1, 3).reshape(AUX_BLK * BLOCK, NOCC, V)
```

```python
import functools

import jax
import jax.numpy as jnp
from jax import lax
from jax.experimental import pallas as pl
from jax.experimental.pallas import tpu as pltpu
from jax.sharding import PartitionSpec as P

BLOCK = 128
NOCC = 8
AUX_BLK = 32
MESH = pl.DeviceIdType.MESH


def pick_energy(occ_energy, column):
    levels = jnp.arange(occ_energy.shape[0], dtype=jnp.int32)
    return jnp.sum(jnp.where(column[:, None] == levels[None, :], occ_energy[None, :], 0.0), axis=1)


def mirror_kernel(side, batches, tile, out, plane, column, s1, r1, s2, r2, s3, r3, own_sem):
    me_a = lax.axis_index("va")
    me_b = lax.axis_index("vb")
    me_p = lax.axis_index("pair")
    size = tile.shape[0] // batches

    def other(base, step):
        return lax.rem(base + step, side)

    barrier = pltpu.get_barrier_semaphore()
    for step in range(1, side):
        pl.semaphore_signal(
            barrier, inc=1, device_id=(other(me_a, step), me_b, me_p), device_id_type=MESH
        )
        pl.semaphore_signal(
            barrier, inc=1, device_id=(me_a, other(me_b, step), me_p), device_id_type=MESH
        )
    pl.semaphore_wait(barrier, 2 * (side - 1))

    def send(src, dst, send_sem, recv_sem, to_a, to_b):
        return pltpu.make_async_remote_copy(
            src_ref=src,
            dst_ref=dst,
            send_sem=send_sem,
            recv_sem=recv_sem,
            device_id=(to_a, to_b, me_p),
            device_id_type=MESH,
        )

    def span(k):
        return pl.ds(k * size, size)

    def first(k, c):
        return send(tile.at[span(k), c], plane.at[me_a, span(k)], s1.at[k, c], r1.at[k, me_a], c, me_b)

    def first_arrival(k, i):
        return send(tile.at[span(k), i], plane.at[i, span(k)], s1.at[k, i], r1.at[k, i], i, me_b)

    def second(k, i, src, direct):
        dst = out.at[span(k), me_a] if direct else column.at[me_b, span(k)]
        return send(src, dst, s2.at[k, i], r2.at[k, me_b], me_a, i)

    def second_arrival(k, j):
        return send(tile.at[span(k), j], column.at[j, span(k)], s2.at[k, j], r2.at[k, j], me_a, j)

    def third(k, j):
        return send(column.at[j, span(k)], out.at[span(k), me_a], s3.at[k, j], r3.at[k, me_a], j, me_b)

    def third_arrival(k, c):
        return send(column.at[c, span(k)], out.at[span(k), c], s3.at[k, c], r3.at[k, c], c, me_b)

    off_diagonal = me_a != me_b

    def start_first(k):
        @pl.when(off_diagonal)
        def _():
            for step in range(1, side):
                first(k, other(me_a, step)).start()

    def start_second(k):
        for step in range(1, side):
            i = other(me_b, step)

            @pl.when(i == me_a)
            def _():
                second(k, i, tile.at[span(k), me_a], False).start()

            @pl.when(i != me_a)
            def _():
                first_arrival(k, i).wait_recv()

                @pl.when(off_diagonal)
                def _():
                    second(k, i, plane.at[i, span(k)], False).start()

                @pl.when(me_a == me_b)
                def _():
                    second(k, i, plane.at[i, span(k)], True).start()

    def start_third(k):
        for step in range(1, side):
            j = other(me_b, step)
            second_arrival(k, j).wait_recv()

            @pl.when(j != me_a)
            def _():
                third(k, j).start()

    own = pltpu.make_async_copy(tile, out, own_sem)

    @pl.when(me_a == me_b)
    def _():
        own.start()

    for k in range(min(2, batches)):
        start_first(k)
    for k in range(batches + 1):
        if k < batches:
            start_second(k)
        if k + 2 < batches:
            start_first(k + 2)
        if k >= 1:
            start_third(k - 1)
    for k in range(batches):

        @pl.when(off_diagonal)
        def _():
            for step in range(1, side):
                c = other(me_a, step)
                third_arrival(k, c).wait_recv()
                first(k, c).wait_send()

        for step in range(1, side):
            i = other(me_b, step)
            second(k, i, tile.at[span(k), me_a], False).wait_send()

            @pl.when(i != me_a)
            def _():
                third(k, i).wait_send()

    @pl.when(me_a == me_b)
    def _():
        own.wait()


def mirror(tile, side):
    pairs, rows, columns = tile.shape
    batches = max(k for k in range(1, 6) if pairs % k == 0)
    strip = rows // side
    cut = jax.ShapeDtypeStruct((pairs, side, strip, columns), tile.dtype)
    held = jax.ShapeDtypeStruct((side, pairs, strip, columns), tile.dtype)
    sems = pltpu.SemaphoreType.DMA((batches, side))
    out, _, _ = pl.pallas_call(
        functools.partial(mirror_kernel, side, batches),
        out_shape=(cut, held, held),
        in_specs=[pl.BlockSpec(memory_space=pl.ANY)],
        out_specs=(pl.BlockSpec(memory_space=pl.ANY),) * 3,
        scratch_shapes=[sems] * 6 + [pltpu.SemaphoreType.DMA],
        compiler_params=pltpu.CompilerParams(collective_id=0, has_side_effects=True),
        name="mirror",
    )(tile.reshape(pairs, side, strip, columns))
    return out.reshape(pairs, rows, columns)


def contract_kernel(dom_blocks, cells, right, amplitude, keep, send, total, staged, keep_sem, send_sem):
    pair = pl.program_id(0)

    @pl.when(pair == 0)
    def _():
        @pl.loop(0, total.shape[0])
        def _(cell):
            total[cell] = jnp.zeros(total.shape[1:], total.dtype)

    for block in range(dom_blocks):
        cell = cells[pair * dom_blocks + block]
        total[cell] += lax.dot_general(
            right[0, :, block * BLOCK : (block + 1) * BLOCK],
            amplitude[0],
            (((0,), (0,)), ((), ())),
            preferred_element_type=jnp.float32,
        )

    @pl.when(pair == pl.num_programs(0) - 1)
    def _():
        half = staged.shape[0]
        keep_copy = pltpu.make_async_copy(total.at[pl.ds(0, half)], keep, keep_sem)
        keep_copy.start()

        @pl.loop(0, half)
        def _(cell):
            staged[cell] = total[half + cell].astype(staged.dtype)

        send_copy = pltpu.make_async_copy(staged, send, send_sem)
        send_copy.start()
        keep_copy.wait()
        send_copy.wait()


def contract(cells, right, amplitude, part, width, send_type):
    pairs, rows, dom = right.shape
    half = AUX_BLK * NOCC // 2
    return pl.pallas_call(
        functools.partial(contract_kernel, dom // BLOCK),
        out_shape=(
            jax.ShapeDtypeStruct((half, BLOCK, width), jnp.float32),
            jax.ShapeDtypeStruct((half, BLOCK, width), send_type),
        ),
        grid_spec=pltpu.PrefetchScalarGridSpec(
            num_scalar_prefetch=1,
            grid=(pairs,),
            in_specs=[
                pl.BlockSpec((1, rows, dom), lambda p, cells: (p, 0, 0)),
                pl.BlockSpec((1, rows, width), lambda p, cells: (p, 0, part)),
            ],
            out_specs=(pl.BlockSpec(memory_space=pl.ANY),) * 2,
            scratch_shapes=[
                pltpu.VMEM((2 * half, BLOCK, width), jnp.float32),
                pltpu.VMEM((half, BLOCK, width), send_type),
                pltpu.SemaphoreType.DMA,
                pltpu.SemaphoreType.DMA,
            ],
        ),
        compiler_params=pltpu.CompilerParams(vmem_limit_bytes=56 << 20),
        cost_estimate=pl.CostEstimate(
            flops=2 * pairs * rows * dom * width,
            bytes_accessed=2 * pairs * rows * (dom + width) + 6 * half * BLOCK * width,
            transcendentals=0,
        ),
        name="contract",
    )(cells, right, amplitude)


def reduce_owned(total_of, count):
    me = lax.axis_index("vb")
    result = total_of(me)
    arrivals = []
    for sign, hops in ((1, count // 2), (-1, (count - 1) // 2)):
        if hops == 0:
            continue
        ring = [(d, (d + sign) % count) for d in range(count)]
        running = total_of((me + sign * hops) % count).astype(jnp.bfloat16)
        for hop in range(1, hops + 1):
            running = lax.ppermute(running, "vb", ring)
            if hop < hops:
                mine = total_of((me + sign * (hops - hop)) % count)
                running = (mine + running.astype(jnp.float32)).astype(jnp.bfloat16)
        arrivals.append(running)
    for arrival in arrivals:
        result = result + arrival.astype(jnp.float32)
    return result


def shards(left_fit, right_fit, occ_energy, virt_energy, pair_list, domain_blocks):
    side = lax.axis_size("va")
    vb_count = lax.axis_size("vb")
    pair_count = lax.axis_size("pair")
    tile_rows = left_fit.shape[1]
    dom_blocks = domain_blocks.shape[1]
    va_index = lax.axis_index("va")
    vb_index = lax.axis_index("vb")
    pair_index = lax.axis_index("pair")
    energy_a = lax.dynamic_slice_in_dim(virt_energy, va_index * tile_rows, tile_rows)
    energy_b = lax.dynamic_slice_in_dim(virt_energy, vb_index * tile_rows, tile_rows)

    coulomb = jnp.einsum(
        "pak,pbk->pab", left_fit, right_fit, preferred_element_type=jnp.float32
    ).astype(jnp.bfloat16)
    swapped = mirror(coulomb, side)
    turned = jnp.swapaxes(coulomb, 1, 2)
    first_energy = pick_energy(occ_energy, pair_list[:, 0])
    second_energy = pick_energy(occ_energy, pair_list[:, 1])
    energy_gap = (
        energy_a[None, None, :] + energy_b[None, :, None] - (first_energy + second_energy)[:, None, None]
    )
    amplitude = (
        (2.0 * turned.astype(jnp.float32) - swapped.astype(jnp.float32)) / energy_gap
    ).astype(jnp.bfloat16)

    slab = AUX_BLK // (vb_count * pair_count)
    owner = domain_blocks // slab
    apart = (owner % pair_count - pair_index) % pair_count
    cells = ((apart * vb_count + owner // pair_count) * slab + domain_blocks % slab) * NOCC
    cells = (cells + pair_list[:, :1]).reshape(-1).astype(jnp.int32)

    send_type = jnp.bfloat16 if vb_count <= 4 else jnp.float32
    parts = max(1, tile_rows // 256)
    width = tile_rows // parts
    swap = [(c, (c + 1) % pair_count) for c in range(pair_count)]
    pieces = []
    for part in range(parts):
        keep, send = contract(cells, right_fit, amplitude, part, width, send_type)
        got = lax.ppermute(send, "pair", swap)
        shape = (vb_count, slab * NOCC, BLOCK, width)
        keep, got = keep.reshape(shape), got.reshape(shape)

        def total_of(owner, keep=keep, got=got):
            mine = lax.dynamic_index_in_dim(keep, owner, 0, False)
            return mine + lax.dynamic_index_in_dim(got, owner, 0, False).astype(jnp.float32)

        mine = reduce_owned(total_of, vb_count).reshape(slab, NOCC, BLOCK, width)
        pieces.append(mine.transpose(0, 2, 1, 3).reshape(slab * BLOCK, NOCC, width))
    return jnp.concatenate(pieces, axis=2)


def solution(mesh):
    return jax.shard_map(
        shards,
        mesh=mesh,
        in_specs=(
            P("pair", "va", None),
            P("pair", "vb", None),
            P(),
            P(),
            P("pair", None),
            P("pair", None),
        ),
        out_specs=P(("vb", "pair"), None, "va"),
        check_vma=False,
    )
```

```python
import functools

import jax
import jax.numpy as jnp
from jax import lax
from jax.experimental import pallas as pl
from jax.experimental.pallas import tpu as pltpu
from jax.sharding import PartitionSpec as P

BLOCK = 128
NOCC = 8
AUX_BLK = 32


def pick_energy(occ_energy, column):
    levels = jnp.arange(occ_energy.shape[0], dtype=jnp.int32)
    return jnp.sum(jnp.where(column[:, None] == levels[None, :], occ_energy[None, :], 0.0), axis=1)


def pick(stack, index):
    return lax.dynamic_index_in_dim(stack, index, 0, False)


def partners(side, step):
    return [(d, d ^ step) for d in range(side)]


def mirror(tile, side):
    pairs, rows, columns = tile.shape
    me_a = lax.axis_index("va")
    me_b = lax.axis_index("vb")
    strips = tile.reshape(pairs, side, rows // side, columns)

    def strip(index):
        return lax.dynamic_index_in_dim(strips, index, 1, False)

    def leg(get, axis):
        held = [get(0)]
        for step in range(1, side):
            held.append(lax.ppermute(get(step), axis, partners(side, step)))
        return jnp.stack(held)

    plane = leg(lambda step: strip(me_a ^ step), "va")
    column = leg(lambda step: pick(plane, me_a ^ me_b ^ step), "vb")
    back = leg(lambda step: pick(column, me_a ^ me_b ^ step), "va")
    ordered = [pick(back, me_a ^ c) for c in range(side)]
    return jnp.stack(ordered, axis=1).reshape(pairs, rows, columns)


def contract_kernel(dom_blocks, cells, right, amplitude, keep, send, total, staged, keep_sem, send_sem):
    pair = pl.program_id(0)

    @pl.when(pair == 0)
    def _():
        @pl.loop(0, total.shape[0])
        def _(cell):
            total[cell] = jnp.zeros(total.shape[1:], total.dtype)

    for block in range(dom_blocks):
        cell = cells[pair * dom_blocks + block]
        total[cell] += lax.dot_general(
            right[0, :, block * BLOCK : (block + 1) * BLOCK],
            amplitude[0],
            (((0,), (0,)), ((), ())),
            preferred_element_type=jnp.float32,
        )

    @pl.when(pair == pl.num_programs(0) - 1)
    def _():
        half = staged.shape[0]
        keep_copy = pltpu.make_async_copy(total.at[pl.ds(0, half)], keep, keep_sem)
        keep_copy.start()

        @pl.loop(0, half)
        def _(cell):
            staged[cell] = total[half + cell].astype(staged.dtype)

        send_copy = pltpu.make_async_copy(staged, send, send_sem)
        send_copy.start()
        keep_copy.wait()
        send_copy.wait()


def contract(cells, right, amplitude, send_type):
    pairs, rows, dom = right.shape
    width = amplitude.shape[2]
    half = AUX_BLK * NOCC // 2
    return pl.pallas_call(
        functools.partial(contract_kernel, dom // BLOCK),
        out_shape=(
            jax.ShapeDtypeStruct((half, BLOCK, width), jnp.float32),
            jax.ShapeDtypeStruct((half, BLOCK, width), send_type),
        ),
        grid_spec=pltpu.PrefetchScalarGridSpec(
            num_scalar_prefetch=1,
            grid=(pairs,),
            in_specs=[
                pl.BlockSpec((1, rows, dom), lambda p, cells: (p, 0, 0)),
                pl.BlockSpec((1, rows, width), lambda p, cells: (p, 0, 0)),
            ],
            out_specs=(pl.BlockSpec(memory_space=pl.ANY),) * 2,
            scratch_shapes=[
                pltpu.VMEM((2 * half, BLOCK, width), jnp.float32),
                pltpu.VMEM((half, BLOCK, width), send_type),
                pltpu.SemaphoreType.DMA,
                pltpu.SemaphoreType.DMA,
            ],
        ),
        compiler_params=pltpu.CompilerParams(vmem_limit_bytes=56 << 20),
        cost_estimate=pl.CostEstimate(
            flops=2 * pairs * rows * dom * width,
            bytes_accessed=2 * pairs * rows * (dom + width) + 6 * half * BLOCK * width,
            transcendentals=0,
        ),
        name="contract",
    )(cells, right, amplitude)


def reduce_owned(total_of, count):
    me = lax.axis_index("vb")
    result = total_of(me)
    arrivals = []
    for sign, hops in ((1, count // 2), (-1, (count - 1) // 2)):
        if hops == 0:
            continue
        ring = [(d, (d + sign) % count) for d in range(count)]
        running = total_of((me + sign * hops) % count).astype(jnp.bfloat16)
        for hop in range(1, hops + 1):
            running = lax.ppermute(running, "vb", ring)
            if hop < hops:
                mine = total_of((me + sign * (hops - hop)) % count)
                running = (mine + running.astype(jnp.float32)).astype(jnp.bfloat16)
        arrivals.append(running)
    for arrival in arrivals:
        result = result + arrival.astype(jnp.float32)
    return result


def shards(left_fit, right_fit, occ_energy, virt_energy, pair_list, domain_blocks):
    side = lax.axis_size("va")
    vb_count = lax.axis_size("vb")
    pair_count = lax.axis_size("pair")
    tile_rows = left_fit.shape[1]
    dom_blocks = domain_blocks.shape[1]
    va_index = lax.axis_index("va")
    vb_index = lax.axis_index("vb")
    pair_index = lax.axis_index("pair")
    energy_a = lax.dynamic_slice_in_dim(virt_energy, va_index * tile_rows, tile_rows)
    energy_b = lax.dynamic_slice_in_dim(virt_energy, vb_index * tile_rows, tile_rows)

    parts = max(1, tile_rows // 256)
    width = tile_rows // parts
    first_energy = pick_energy(occ_energy, pair_list[:, 0])
    second_energy = pick_energy(occ_energy, pair_list[:, 1])
    pair_energy = (first_energy + second_energy)[:, None, None]
    tiles = []
    for part in range(parts):
        columns = right_fit[:, part * width : (part + 1) * width]
        tile = jnp.einsum("pak,pbk->pab", left_fit, columns, preferred_element_type=jnp.float32)
        tiles.append(tile.astype(jnp.bfloat16))
    mirrored = [mirror(tile, side) for tile in tiles]

    def amplitude_of(part):
        rows = slice(part * width, (part + 1) * width)
        turned = jnp.einsum(
            "pbk,pak->pba", right_fit, left_fit[:, rows], preferred_element_type=jnp.float32
        ).astype(jnp.bfloat16)
        energy_gap = energy_a[None, None, rows] + energy_b[None, :, None] - pair_energy
        wide = 2.0 * turned.astype(jnp.float32) - mirrored[part].astype(jnp.float32)
        return (wide / energy_gap).astype(jnp.bfloat16)

    slab = AUX_BLK // (vb_count * pair_count)
    owner = domain_blocks // slab
    apart = (owner % pair_count - pair_index) % pair_count
    cells = ((apart * vb_count + owner // pair_count) * slab + domain_blocks % slab) * NOCC
    cells = (cells + pair_list[:, :1]).reshape(-1).astype(jnp.int32)

    send_type = jnp.bfloat16 if vb_count <= 4 else jnp.float32
    swap = [(c, (c + 1) % pair_count) for c in range(pair_count)]
    pieces = []
    for part in range(parts):
        keep, send = contract(cells, right_fit, amplitude_of(part), send_type)
        got = lax.ppermute(send, "pair", swap)
        shape = (vb_count, slab * NOCC, BLOCK, width)
        keep, got = keep.reshape(shape), got.reshape(shape)

        def total_of(owner, keep=keep, got=got):
            mine = lax.dynamic_index_in_dim(keep, owner, 0, False)
            return mine + lax.dynamic_index_in_dim(got, owner, 0, False).astype(jnp.float32)

        mine = reduce_owned(total_of, vb_count).reshape(slab, NOCC, BLOCK, width)
        pieces.append(mine.transpose(0, 2, 1, 3).reshape(slab * BLOCK, NOCC, width))
    return jnp.concatenate(pieces, axis=2)


def solution(mesh):
    return jax.shard_map(
        shards,
        mesh=mesh,
        in_specs=(
            P("pair", "va", None),
            P("pair", "vb", None),
            P(),
            P(),
            P("pair", None),
            P("pair", None),
        ),
        out_specs=P(("vb", "pair"), None, "va"),
        check_vma=False,
    )
```

```python
import functools

import jax
import jax.numpy as jnp
from jax import lax
from jax.experimental import pallas as pl
from jax.experimental.pallas import tpu as pltpu
from jax.sharding import PartitionSpec as P

BLOCK = 128
NOCC = 8
AUX_BLK = 32


def pick_energy(occ_energy, column):
    levels = jnp.arange(occ_energy.shape[0], dtype=jnp.int32)
    return jnp.sum(jnp.where(column[:, None] == levels[None, :], occ_energy[None, :], 0.0), axis=1)


def pick(stack, index):
    return lax.dynamic_index_in_dim(stack, index, 0, False)


def partners(side, step):
    return [(d, d ^ step) for d in range(side)]


def leg(get, side, axis):
    held = [get(0)]
    for step in range(1, side):
        held.append(lax.ppermute(get(step), axis, partners(side, step)))
    return held


def first_leg(tile, side):
    pairs, rows, columns = tile.shape
    me_a = lax.axis_index("va")
    strips = tile.reshape(pairs, side, rows // side, columns)
    return leg(
        lambda step: lax.dynamic_index_in_dim(strips, me_a ^ step, 1, False), side, "va"
    )


def next_leg(held, axis):
    apart = lax.axis_index("va") ^ lax.axis_index("vb")
    stack = jnp.stack(held)
    return leg(lambda step: pick(stack, apart ^ step), len(held), axis)


def assemble(held):
    pairs, strip, columns = held[0].shape
    me_a = lax.axis_index("va")
    stack = jnp.stack(held)
    ordered = [pick(stack, me_a ^ c) for c in range(len(held))]
    return jnp.stack(ordered, axis=1).reshape(pairs, len(held) * strip, columns)


def contract_kernel(dom_blocks, cells, right, amplitude, keep, send, total, staged, keep_sem, send_sem):
    pair = pl.program_id(0)

    @pl.when(pair == 0)
    def _():
        @pl.loop(0, total.shape[0])
        def _(cell):
            total[cell] = jnp.zeros(total.shape[1:], total.dtype)

    for block in range(dom_blocks):
        cell = cells[pair * dom_blocks + block]
        total[cell] += lax.dot_general(
            right[0, :, block * BLOCK : (block + 1) * BLOCK],
            amplitude[0],
            (((0,), (0,)), ((), ())),
            preferred_element_type=jnp.float32,
        )

    @pl.when(pair == pl.num_programs(0) - 1)
    def _():
        half = staged.shape[0]
        keep_copy = pltpu.make_async_copy(total.at[pl.ds(0, half)], keep, keep_sem)
        keep_copy.start()

        @pl.loop(0, half)
        def _(cell):
            staged[cell] = total[half + cell].astype(staged.dtype)

        send_copy = pltpu.make_async_copy(staged, send, send_sem)
        send_copy.start()
        keep_copy.wait()
        send_copy.wait()


def contract(cells, right, amplitude, send_type):
    pairs, rows, dom = right.shape
    width = amplitude.shape[2]
    half = AUX_BLK * NOCC // 2
    return pl.pallas_call(
        functools.partial(contract_kernel, dom // BLOCK),
        out_shape=(
            jax.ShapeDtypeStruct((half, BLOCK, width), jnp.float32),
            jax.ShapeDtypeStruct((half, BLOCK, width), send_type),
        ),
        grid_spec=pltpu.PrefetchScalarGridSpec(
            num_scalar_prefetch=1,
            grid=(pairs,),
            in_specs=[
                pl.BlockSpec((1, rows, dom), lambda p, cells: (p, 0, 0)),
                pl.BlockSpec((1, rows, width), lambda p, cells: (p, 0, 0)),
            ],
            out_specs=(pl.BlockSpec(memory_space=pl.ANY),) * 2,
            scratch_shapes=[
                pltpu.VMEM((2 * half, BLOCK, width), jnp.float32),
                pltpu.VMEM((half, BLOCK, width), send_type),
                pltpu.SemaphoreType.DMA,
                pltpu.SemaphoreType.DMA,
            ],
        ),
        compiler_params=pltpu.CompilerParams(vmem_limit_bytes=56 << 20),
        cost_estimate=pl.CostEstimate(
            flops=2 * pairs * rows * dom * width,
            bytes_accessed=2 * pairs * rows * (dom + width) + 6 * half * BLOCK * width,
            transcendentals=0,
        ),
        name="contract",
    )(cells, right, amplitude)


def ring(count, sign):
    return [(d, (d + sign) % count) for d in range(count)]


def ways(count):
    return [(sign, hops) for sign, hops in ((1, count // 2), (-1, (count - 1) // 2)) if hops]


def first_sums(total_of, count):
    me = lax.axis_index("vb")
    return [total_of((me + sign * hops) % count).astype(jnp.bfloat16) for sign, hops in ways(count)]


def first_hops(sums, count):
    return [lax.ppermute(x, "vb", ring(count, sign)) for x, (sign, _) in zip(sums, ways(count))]


def last_hops(total_of, arrivals, count):
    me = lax.axis_index("vb")
    arrived = []
    for running, (sign, hops) in zip(arrivals, ways(count)):
        for hop in range(1, hops):
            mine = total_of((me + sign * (hops - hop)) % count)
            running = (mine + running.astype(jnp.float32)).astype(jnp.bfloat16)
            running = lax.ppermute(running, "vb", ring(count, sign))
        arrived.append(running)
    return arrived


def shards(left_fit, right_fit, occ_energy, virt_energy, pair_list, domain_blocks):
    side = lax.axis_size("va")
    vb_count = lax.axis_size("vb")
    pair_count = lax.axis_size("pair")
    tile_rows = left_fit.shape[1]
    dom_blocks = domain_blocks.shape[1]
    va_index = lax.axis_index("va")
    vb_index = lax.axis_index("vb")
    pair_index = lax.axis_index("pair")
    energy_a = lax.dynamic_slice_in_dim(virt_energy, va_index * tile_rows, tile_rows)
    energy_b = lax.dynamic_slice_in_dim(virt_energy, vb_index * tile_rows, tile_rows)

    parts = max(1, tile_rows // 256)
    width = tile_rows // parts
    first_energy = pick_energy(occ_energy, pair_list[:, 0])
    second_energy = pick_energy(occ_energy, pair_list[:, 1])
    pair_energy = (first_energy + second_energy)[:, None, None]
    tiles = []
    for part in range(parts):
        columns = right_fit[:, part * width : (part + 1) * width]
        tile = jnp.einsum("pak,pbk->pab", left_fit, columns, preferred_element_type=jnp.float32)
        tiles.append(tile.astype(jnp.bfloat16))
    turned = []
    for part in range(parts):
        rows = left_fit[:, part * width : (part + 1) * width]
        tile = jnp.einsum("pbk,pak->pba", right_fit, rows, preferred_element_type=jnp.float32)
        turned.append(tile.astype(jnp.bfloat16))

    plane, column = [], []
    for part in range(parts):
        tile = tiles[part]
        if part:
            tile, plane[-1], turned[0] = lax.optimization_barrier((tile, plane[-1], turned[0]))
        plane.append(first_leg(tile, side))
    for part in range(parts):
        if part:
            plane[part], column[-1], turned[part] = lax.optimization_barrier(
                (plane[part], column[-1], turned[part])
            )
        column.append(next_leg(plane[part], "vb"))

    def amplitude_of(part):
        mirrored = assemble(next_leg(column[part], "va"))
        rows = slice(part * width, (part + 1) * width)
        energy_gap = energy_a[None, None, rows] + energy_b[None, :, None] - pair_energy
        wide = 2.0 * turned[part].astype(jnp.float32) - mirrored.astype(jnp.float32)
        return (wide / energy_gap).astype(jnp.bfloat16)

    slab = AUX_BLK // (vb_count * pair_count)
    owner = domain_blocks // slab
    apart = (owner % pair_count - pair_index) % pair_count
    cells = ((apart * vb_count + owner // pair_count) * slab + domain_blocks % slab) * NOCC
    cells = (cells + pair_list[:, :1]).reshape(-1).astype(jnp.int32)

    send_type = jnp.bfloat16 if vb_count <= 4 else jnp.float32
    swap = [(c, (c + 1) % pair_count) for c in range(pair_count)]
    shape = (vb_count, slab * NOCC, BLOCK, width)
    totals, hops = [], []
    for part in range(parts):
        keep, send = contract(cells, right_fit, amplitude_of(part), send_type)
        if part:
            send, hops[-1] = lax.optimization_barrier((send, hops[-1]))
        got = lax.ppermute(send, "pair", swap)
        keep, got = keep.reshape(shape), got.reshape(shape)

        def total_of(owner, keep=keep, got=got):
            return pick(keep, owner) + pick(got, owner).astype(jnp.float32)

        totals.append(total_of)
        sums = first_sums(total_of, vb_count)
        if part + 1 < parts:
            sums, column[part + 1] = lax.optimization_barrier((sums, column[part + 1]))
        hops.append(first_hops(sums, vb_count))
    pieces = []
    for part in range(parts):
        arrived = last_hops(totals[part], hops[part], vb_count)
        if part:
            arrived, pieces[-1] = lax.optimization_barrier((arrived, pieces[-1]))
        mine = totals[part](vb_index)
        for arrival in arrived:
            mine = mine + arrival.astype(jnp.float32)
        mine = mine.reshape(slab, NOCC, BLOCK, width)
        pieces.append(mine.transpose(0, 2, 1, 3).reshape(slab * BLOCK, NOCC, width))
    return jnp.concatenate(pieces, axis=2)


def solution(mesh):
    return jax.shard_map(
        shards,
        mesh=mesh,
        in_specs=(
            P("pair", "va", None),
            P("pair", "vb", None),
            P(),
            P(),
            P("pair", None),
            P("pair", None),
        ),
        out_specs=P(("vb", "pair"), None, "va"),
        check_vma=False,
    )
```

```python
import functools

import jax
import jax.numpy as jnp
from jax import lax
from jax.experimental import pallas as pl
from jax.experimental.pallas import tpu as pltpu
from jax.sharding import PartitionSpec as P

BLOCK = 128
NOCC = 8
AUX_BLK = 32


def pick_energy(occ_energy, column):
    levels = jnp.arange(occ_energy.shape[0], dtype=jnp.int32)
    return jnp.sum(jnp.where(column[:, None] == levels[None, :], occ_energy[None, :], 0.0), axis=1)


def pick(stack, index):
    return lax.dynamic_index_in_dim(stack, index, 0, False)


def partners(side, step):
    return [(d, d ^ step) for d in range(side)]


def leg(get, side, axis):
    held = [get(0)]
    for step in range(1, side):
        held.append(lax.ppermute(get(step), axis, partners(side, step)))
    return held


def first_leg(tile, side):
    pairs, rows, columns = tile.shape
    me_a = lax.axis_index("va")
    strips = tile.reshape(pairs, side, rows // side, columns)
    return leg(
        lambda step: lax.dynamic_index_in_dim(strips, me_a ^ step, 1, False), side, "va"
    )


def next_leg(held, axis):
    apart = lax.axis_index("va") ^ lax.axis_index("vb")
    stack = jnp.stack(held)
    return leg(lambda step: pick(stack, apart ^ step), len(held), axis)


def assemble(held):
    pairs, strip, columns = held[0].shape
    me_a = lax.axis_index("va")
    stack = jnp.stack(held)
    ordered = [pick(stack, me_a ^ c) for c in range(len(held))]
    return jnp.stack(ordered, axis=1).reshape(pairs, len(held) * strip, columns)


def contract_kernel(dom_blocks, cells, right, amplitude, keep, send, total, staged, keep_sem, send_sem):
    pair = pl.program_id(0)

    @pl.when(pair == 0)
    def _():
        @pl.loop(0, total.shape[0])
        def _(cell):
            total[cell] = jnp.zeros(total.shape[1:], total.dtype)

    for block in range(dom_blocks):
        cell = cells[pair * dom_blocks + block]
        total[cell] += lax.dot_general(
            right[0, :, block * BLOCK : (block + 1) * BLOCK],
            amplitude[0],
            (((0,), (0,)), ((), ())),
            preferred_element_type=jnp.float32,
        )

    @pl.when(pair == pl.num_programs(0) - 1)
    def _():
        half = staged.shape[0]
        keep_copy = pltpu.make_async_copy(total.at[pl.ds(0, half)], keep, keep_sem)
        keep_copy.start()

        @pl.loop(0, half)
        def _(cell):
            staged[cell] = total[half + cell].astype(staged.dtype)

        send_copy = pltpu.make_async_copy(staged, send, send_sem)
        send_copy.start()
        keep_copy.wait()
        send_copy.wait()


def contract(cells, right, amplitude, send_type):
    pairs, rows, dom = right.shape
    width = amplitude.shape[2]
    half = AUX_BLK * NOCC // 2
    return pl.pallas_call(
        functools.partial(contract_kernel, dom // BLOCK),
        out_shape=(
            jax.ShapeDtypeStruct((half, BLOCK, width), jnp.float32),
            jax.ShapeDtypeStruct((half, BLOCK, width), send_type),
        ),
        grid_spec=pltpu.PrefetchScalarGridSpec(
            num_scalar_prefetch=1,
            grid=(pairs,),
            in_specs=[
                pl.BlockSpec((1, rows, dom), lambda p, cells: (p, 0, 0)),
                pl.BlockSpec((1, rows, width), lambda p, cells: (p, 0, 0)),
            ],
            out_specs=(pl.BlockSpec(memory_space=pl.ANY),) * 2,
            scratch_shapes=[
                pltpu.VMEM((2 * half, BLOCK, width), jnp.float32),
                pltpu.VMEM((half, BLOCK, width), send_type),
                pltpu.SemaphoreType.DMA,
                pltpu.SemaphoreType.DMA,
            ],
        ),
        compiler_params=pltpu.CompilerParams(vmem_limit_bytes=56 << 20),
        cost_estimate=pl.CostEstimate(
            flops=2 * pairs * rows * dom * width,
            bytes_accessed=2 * pairs * rows * (dom + width) + 6 * half * BLOCK * width,
            transcendentals=0,
        ),
        name="contract",
    )(cells, right, amplitude)


def ring(count, sign):
    return [(d, (d + sign) % count) for d in range(count)]


def ways(count):
    return [(sign, hops) for sign, hops in ((1, count // 2), (-1, (count - 1) // 2)) if hops]


def first_sums(total_of, count):
    me = lax.axis_index("vb")
    return [total_of((me + sign * hops) % count).astype(jnp.bfloat16) for sign, hops in ways(count)]


def first_hops(sums, count):
    return [lax.ppermute(x, "vb", ring(count, sign)) for x, (sign, _) in zip(sums, ways(count))]


def last_hops(total_of, arrivals, count):
    me = lax.axis_index("vb")
    arrived = []
    for running, (sign, hops) in zip(arrivals, ways(count)):
        for hop in range(1, hops):
            mine = total_of((me + sign * (hops - hop)) % count)
            running = (mine + running.astype(jnp.float32)).astype(jnp.bfloat16)
            running = lax.ppermute(running, "vb", ring(count, sign))
        arrived.append(running)
    return arrived


def shards(left_fit, right_fit, occ_energy, virt_energy, pair_list, domain_blocks):
    side = lax.axis_size("va")
    vb_count = lax.axis_size("vb")
    pair_count = lax.axis_size("pair")
    tile_rows = left_fit.shape[1]
    dom_blocks = domain_blocks.shape[1]
    va_index = lax.axis_index("va")
    vb_index = lax.axis_index("vb")
    pair_index = lax.axis_index("pair")
    energy_a = lax.dynamic_slice_in_dim(virt_energy, va_index * tile_rows, tile_rows)
    energy_b = lax.dynamic_slice_in_dim(virt_energy, vb_index * tile_rows, tile_rows)

    parts = max(1, tile_rows // 256)
    width = tile_rows // parts
    first_energy = pick_energy(occ_energy, pair_list[:, 0])
    second_energy = pick_energy(occ_energy, pair_list[:, 1])
    pair_energy = (first_energy + second_energy)[:, None, None]
    tiles = []
    for part in range(parts):
        columns = right_fit[:, part * width : (part + 1) * width]
        tile = jnp.einsum("pak,pbk->pab", left_fit, columns, preferred_element_type=jnp.float32)
        tiles.append(tile.astype(jnp.bfloat16))
    turned = []
    for part in range(parts):
        rows = left_fit[:, part * width : (part + 1) * width]
        tile = jnp.einsum("pbk,pak->pba", right_fit, rows, preferred_element_type=jnp.float32)
        turned.append(tile.astype(jnp.bfloat16))

    plane, column = [], []
    for part in range(parts):
        tile = tiles[part]
        if part:
            tile, plane[-1], turned[0] = lax.optimization_barrier((tile, plane[-1], turned[0]))
        plane.append(first_leg(tile, side))
    for part in range(parts):
        if part:
            plane[part], column[-1], turned[part] = lax.optimization_barrier(
                (plane[part], column[-1], turned[part])
            )
        column.append(next_leg(plane[part], "vb"))

    def amplitude_of(part):
        back = next_leg(column[part], "va")
        if part + 1 < parts:
            back, column[part + 1][:-1] = lax.optimization_barrier((back, column[part + 1][:-1]))
        mirrored = assemble(back)
        rows = slice(part * width, (part + 1) * width)
        energy_gap = energy_a[None, None, rows] + energy_b[None, :, None] - pair_energy
        wide = 2.0 * turned[part].astype(jnp.float32) - mirrored.astype(jnp.float32)
        return (wide / energy_gap).astype(jnp.bfloat16)

    slab = AUX_BLK // (vb_count * pair_count)
    owner = domain_blocks // slab
    apart = (owner % pair_count - pair_index) % pair_count
    cells = ((apart * vb_count + owner // pair_count) * slab + domain_blocks % slab) * NOCC
    cells = (cells + pair_list[:, :1]).reshape(-1).astype(jnp.int32)

    send_type = jnp.bfloat16 if vb_count <= 4 else jnp.float32
    swap = [(c, (c + 1) % pair_count) for c in range(pair_count)]
    shape = (vb_count, slab * NOCC, BLOCK, width)
    totals, hops = [], []
    for part in range(parts):
        keep, send = contract(cells, right_fit, amplitude_of(part), send_type)
        if part:
            send, hops[-1] = lax.optimization_barrier((send, hops[-1]))
        if part + 1 < parts:
            send, column[part + 1][-1] = lax.optimization_barrier((send, column[part + 1][-1]))
        got = lax.ppermute(send, "pair", swap)
        keep, got = keep.reshape(shape), got.reshape(shape)

        def total_of(owner, keep=keep, got=got):
            return pick(keep, owner) + pick(got, owner).astype(jnp.float32)

        totals.append(total_of)
        sums = first_sums(total_of, vb_count)
        if part + 1 < parts:
            sums, column[part + 1] = lax.optimization_barrier((sums, column[part + 1]))
        hops.append(first_hops(sums, vb_count))
    pieces = []
    for part in range(parts):
        arrived = last_hops(totals[part], hops[part], vb_count)
        if part:
            arrived, pieces[-1] = lax.optimization_barrier((arrived, pieces[-1]))
        mine = totals[part](vb_index)
        for arrival in arrived:
            mine = mine + arrival.astype(jnp.float32)
        mine = mine.reshape(slab, NOCC, BLOCK, width)
        pieces.append(mine.transpose(0, 2, 1, 3).reshape(slab * BLOCK, NOCC, width))
    return jnp.concatenate(pieces, axis=2)


def solution(mesh):
    return jax.shard_map(
        shards,
        mesh=mesh,
        in_specs=(
            P("pair", "va", None),
            P("pair", "vb", None),
            P(),
            P(),
            P("pair", None),
            P("pair", None),
        ),
        out_specs=P(("vb", "pair"), None, "va"),
        check_vma=False,
    )
```

```python
import functools

import jax
import jax.numpy as jnp
from jax import lax
from jax.experimental import pallas as pl
from jax.experimental.pallas import tpu as pltpu
from jax.sharding import PartitionSpec as P

BLOCK = 128
NOCC = 8
AUX_BLK = 32


def pick_energy(occ_energy, column):
    levels = jnp.arange(occ_energy.shape[0], dtype=jnp.int32)
    return jnp.sum(jnp.where(column[:, None] == levels[None, :], occ_energy[None, :], 0.0), axis=1)


def pick(stack, index):
    return lax.dynamic_index_in_dim(stack, index, 0, False)


def partners(side, step):
    return [(d, d ^ step) for d in range(side)]


def leg(get, side, axis):
    held = [get(0)]
    for step in range(1, side):
        held.append(lax.ppermute(get(step), axis, partners(side, step)))
    return held


def first_leg(tile, side):
    pairs, rows, columns = tile.shape
    me_a = lax.axis_index("va")
    strips = tile.reshape(pairs, side, rows // side, columns)
    return leg(
        lambda step: lax.dynamic_index_in_dim(strips, me_a ^ step, 1, False), side, "va"
    )


def next_leg(held, axis):
    apart = lax.axis_index("va") ^ lax.axis_index("vb")
    stack = jnp.stack(held)
    return leg(lambda step: pick(stack, apart ^ step), len(held), axis)


def assemble(held):
    pairs, strip, columns = held[0].shape
    me_a = lax.axis_index("va")
    stack = jnp.stack(held)
    ordered = [pick(stack, me_a ^ c) for c in range(len(held))]
    return jnp.stack(ordered, axis=1).reshape(pairs, len(held) * strip, columns)


def contract_kernel(dom_blocks, cells, right, amplitude, keep, send, total, staged, keep_sem, send_sem):
    pair = pl.program_id(0)

    @pl.when(pair == 0)
    def _():
        @pl.loop(0, total.shape[0])
        def _(cell):
            total[cell] = jnp.zeros(total.shape[1:], total.dtype)

    for block in range(dom_blocks):
        cell = cells[pair * dom_blocks + block]
        total[cell] += lax.dot_general(
            right[0, :, block * BLOCK : (block + 1) * BLOCK],
            amplitude[0],
            (((0,), (0,)), ((), ())),
            preferred_element_type=jnp.float32,
        )

    @pl.when(pair == pl.num_programs(0) - 1)
    def _():
        half = staged.shape[0]
        keep_copy = pltpu.make_async_copy(total.at[pl.ds(0, half)], keep, keep_sem)
        keep_copy.start()

        @pl.loop(0, half)
        def _(cell):
            staged[cell] = total[half + cell].astype(staged.dtype)

        send_copy = pltpu.make_async_copy(staged, send, send_sem)
        send_copy.start()
        keep_copy.wait()
        send_copy.wait()


def contract(cells, right, amplitude, send_type):
    pairs, rows, dom = right.shape
    width = amplitude.shape[2]
    half = AUX_BLK * NOCC // 2
    return pl.pallas_call(
        functools.partial(contract_kernel, dom // BLOCK),
        out_shape=(
            jax.ShapeDtypeStruct((half, BLOCK, width), jnp.float32),
            jax.ShapeDtypeStruct((half, BLOCK, width), send_type),
        ),
        grid_spec=pltpu.PrefetchScalarGridSpec(
            num_scalar_prefetch=1,
            grid=(pairs,),
            in_specs=[
                pl.BlockSpec((1, rows, dom), lambda p, cells: (p, 0, 0)),
                pl.BlockSpec((1, rows, width), lambda p, cells: (p, 0, 0)),
            ],
            out_specs=(pl.BlockSpec(memory_space=pl.ANY),) * 2,
            scratch_shapes=[
                pltpu.VMEM((2 * half, BLOCK, width), jnp.float32),
                pltpu.VMEM((half, BLOCK, width), send_type),
                pltpu.SemaphoreType.DMA,
                pltpu.SemaphoreType.DMA,
            ],
        ),
        compiler_params=pltpu.CompilerParams(vmem_limit_bytes=56 << 20),
        cost_estimate=pl.CostEstimate(
            flops=2 * pairs * rows * dom * width,
            bytes_accessed=2 * pairs * rows * (dom + width) + 6 * half * BLOCK * width,
            transcendentals=0,
        ),
        name="contract",
    )(cells, right, amplitude)


def ring(count, sign):
    return [(d, (d + sign) % count) for d in range(count)]


def ways(count):
    return [(sign, hops) for sign, hops in ((1, count // 2), (-1, (count - 1) // 2)) if hops]


def hop_sums(total_of, arrivals, hop, count):
    me = lax.axis_index("vb")
    sums = []
    for way, (sign, hops) in enumerate(ways(count)):
        if hop >= hops:
            sums.append(None)
            continue
        mine = total_of((me + sign * (hops - hop)) % count)
        if hop:
            mine = mine + arrivals[way].astype(jnp.float32)
        sums.append(mine.astype(jnp.bfloat16))
    return sums


def make_hop(sums, arrivals, count):
    made = []
    for way, (sign, _) in enumerate(ways(count)):
        going = sums[way]
        made.append(arrivals[way] if going is None else lax.ppermute(going, "vb", ring(count, sign)))
    return made


def shards(left_fit, right_fit, occ_energy, virt_energy, pair_list, domain_blocks):
    side = lax.axis_size("va")
    vb_count = lax.axis_size("vb")
    pair_count = lax.axis_size("pair")
    tile_rows = left_fit.shape[1]
    dom_blocks = domain_blocks.shape[1]
    va_index = lax.axis_index("va")
    vb_index = lax.axis_index("vb")
    pair_index = lax.axis_index("pair")
    energy_a = lax.dynamic_slice_in_dim(virt_energy, va_index * tile_rows, tile_rows)
    energy_b = lax.dynamic_slice_in_dim(virt_energy, vb_index * tile_rows, tile_rows)

    parts = max(1, tile_rows // 256)
    width = tile_rows // parts
    first_energy = pick_energy(occ_energy, pair_list[:, 0])
    second_energy = pick_energy(occ_energy, pair_list[:, 1])
    pair_energy = (first_energy + second_energy)[:, None, None]
    tiles = []
    for part in range(parts):
        columns = right_fit[:, part * width : (part + 1) * width]
        tile = jnp.einsum("pak,pbk->pab", left_fit, columns, preferred_element_type=jnp.float32)
        tiles.append(tile.astype(jnp.bfloat16))
    turned = []
    for part in range(parts):
        rows = left_fit[:, part * width : (part + 1) * width]
        tile = jnp.einsum("pbk,pak->pba", right_fit, rows, preferred_element_type=jnp.float32)
        turned.append(tile.astype(jnp.bfloat16))

    plane, column = [], []
    for part in range(parts):
        tile = tiles[part]
        if part:
            tile, plane[-1], turned[0] = lax.optimization_barrier((tile, plane[-1], turned[0]))
        plane.append(first_leg(tile, side))
    for part in range(parts):
        if part:
            plane[part], column[-1], turned[part] = lax.optimization_barrier(
                (plane[part], column[-1], turned[part])
            )
        column.append(next_leg(plane[part], "vb"))

    def amplitude_of(part):
        back = next_leg(column[part], "va")
        if part + 1 < parts:
            back, column[part + 1][:2] = lax.optimization_barrier((back, column[part + 1][:2]))
        mirrored = assemble(back)
        rows = slice(part * width, (part + 1) * width)
        energy_gap = energy_a[None, None, rows] + energy_b[None, :, None] - pair_energy
        wide = 2.0 * turned[part].astype(jnp.float32) - mirrored.astype(jnp.float32)
        return (wide / energy_gap).astype(jnp.bfloat16)

    slab = AUX_BLK // (vb_count * pair_count)
    owner = domain_blocks // slab
    apart = (owner % pair_count - pair_index) % pair_count
    cells = ((apart * vb_count + owner // pair_count) * slab + domain_blocks % slab) * NOCC
    cells = (cells + pair_list[:, :1]).reshape(-1).astype(jnp.int32)

    send_type = jnp.bfloat16 if vb_count <= 4 else jnp.float32
    swap = [(c, (c + 1) % pair_count) for c in range(pair_count)]
    shape = (vb_count, slab * NOCC, BLOCK, width)
    totals, hops = [], []
    for part in range(parts):
        keep, send = contract(cells, right_fit, amplitude_of(part), send_type)
        if part:
            send, hops[-1] = lax.optimization_barrier((send, hops[-1]))
            sums = hop_sums(totals[-1], hops[-1], 1, vb_count)
            send, sums = lax.optimization_barrier((send, sums))
            hops[-1] = make_hop(sums, hops[-1], vb_count)
        if part + 1 < parts:
            send, column[part + 1][2:] = lax.optimization_barrier((send, column[part + 1][2:]))
        got = lax.ppermute(send, "pair", swap)
        keep, got = keep.reshape(shape), got.reshape(shape)

        def total_of(owner, keep=keep, got=got):
            return pick(keep, owner) + pick(got, owner).astype(jnp.float32)

        totals.append(total_of)
        sums = hop_sums(total_of, None, 0, vb_count)
        if part:
            sums, hops[-1] = lax.optimization_barrier((sums, hops[-1]))
        if part + 1 < parts:
            sums, column[part + 1] = lax.optimization_barrier((sums, column[part + 1]))
        hops.append(make_hop(sums, None, vb_count))
    pieces = []
    for part in range(parts):
        arrived = hops[part]
        for hop in range(2 if part + 1 < parts else 1, vb_count // 2):
            arrived = make_hop(hop_sums(totals[part], arrived, hop, vb_count), arrived, vb_count)
        if part:
            arrived, pieces[-1] = lax.optimization_barrier((arrived, pieces[-1]))
        mine = totals[part](vb_index)
        for arrival in arrived:
            mine = mine + arrival.astype(jnp.float32)
        mine = mine.reshape(slab, NOCC, BLOCK, width)
        pieces.append(mine.transpose(0, 2, 1, 3).reshape(slab * BLOCK, NOCC, width))
    return jnp.concatenate(pieces, axis=2)


def solution(mesh):
    return jax.shard_map(
        shards,
        mesh=mesh,
        in_specs=(
            P("pair", "va", None),
            P("pair", "vb", None),
            P(),
            P(),
            P("pair", None),
            P("pair", None),
        ),
        out_specs=P(("vb", "pair"), None, "va"),
        check_vma=False,
    )
```

```python
import functools

import jax
import jax.numpy as jnp
from jax import lax
from jax.experimental import pallas as pl
from jax.experimental.pallas import tpu as pltpu
from jax.sharding import PartitionSpec as P

BLOCK = 128
NOCC = 8
AUX_BLK = 32


def pick_energy(occ_energy, column):
    levels = jnp.arange(occ_energy.shape[0], dtype=jnp.int32)
    return jnp.sum(jnp.where(column[:, None] == levels[None, :], occ_energy[None, :], 0.0), axis=1)


def pick(stack, index):
    return lax.dynamic_index_in_dim(stack, index, 0, False)


def partners(side, step):
    return [(d, d ^ step) for d in range(side)]


def leg(get, side, axis):
    held = [get(0)]
    for step in range(1, side):
        held.append(lax.ppermute(get(step), axis, partners(side, step)))
    return held


def first_leg(tile, side):
    pairs, rows, columns = tile.shape
    me_a = lax.axis_index("va")
    strips = tile.reshape(pairs, side, rows // side, columns)
    return leg(
        lambda step: lax.dynamic_index_in_dim(strips, me_a ^ step, 1, False), side, "va"
    )


def next_leg(held, axis):
    apart = lax.axis_index("va") ^ lax.axis_index("vb")
    stack = jnp.stack(held)
    return leg(lambda step: pick(stack, apart ^ step), len(held), axis)


def assemble(held):
    pairs, strip, columns = held[0].shape
    me_a = lax.axis_index("va")
    stack = jnp.stack(held)
    ordered = [pick(stack, me_a ^ c) for c in range(len(held))]
    return jnp.stack(ordered, axis=1).reshape(pairs, len(held) * strip, columns)


def contract_kernel(dom_blocks, cells, right, amplitude, keep, send, total, staged, keep_sem, send_sem):
    pair = pl.program_id(0)

    @pl.when(pair == 0)
    def _():
        @pl.loop(0, total.shape[0])
        def _(cell):
            total[cell] = jnp.zeros(total.shape[1:], total.dtype)

    for block in range(dom_blocks):
        cell = cells[pair * dom_blocks + block]
        total[cell] += lax.dot_general(
            right[0, :, block * BLOCK : (block + 1) * BLOCK],
            amplitude[0],
            (((0,), (0,)), ((), ())),
            preferred_element_type=jnp.float32,
        )

    @pl.when(pair == pl.num_programs(0) - 1)
    def _():
        half = staged.shape[0]
        keep_copy = pltpu.make_async_copy(total.at[pl.ds(0, half)], keep, keep_sem)
        keep_copy.start()

        @pl.loop(0, half)
        def _(cell):
            staged[cell] = total[half + cell].astype(staged.dtype)

        send_copy = pltpu.make_async_copy(staged, send, send_sem)
        send_copy.start()
        keep_copy.wait()
        send_copy.wait()


def contract(cells, right, amplitude, send_type):
    pairs, rows, dom = right.shape
    width = amplitude.shape[2]
    half = AUX_BLK * NOCC // 2
    return pl.pallas_call(
        functools.partial(contract_kernel, dom // BLOCK),
        out_shape=(
            jax.ShapeDtypeStruct((half, BLOCK, width), jnp.float32),
            jax.ShapeDtypeStruct((half, BLOCK, width), send_type),
        ),
        grid_spec=pltpu.PrefetchScalarGridSpec(
            num_scalar_prefetch=1,
            grid=(pairs,),
            in_specs=[
                pl.BlockSpec((1, rows, dom), lambda p, cells: (p, 0, 0)),
                pl.BlockSpec((1, rows, width), lambda p, cells: (p, 0, 0)),
            ],
            out_specs=(pl.BlockSpec(memory_space=pl.ANY),) * 2,
            scratch_shapes=[
                pltpu.VMEM((2 * half, BLOCK, width), jnp.float32),
                pltpu.VMEM((half, BLOCK, width), send_type),
                pltpu.SemaphoreType.DMA,
                pltpu.SemaphoreType.DMA,
            ],
        ),
        compiler_params=pltpu.CompilerParams(vmem_limit_bytes=56 << 20),
        cost_estimate=pl.CostEstimate(
            flops=2 * pairs * rows * dom * width,
            bytes_accessed=2 * pairs * rows * (dom + width) + 6 * half * BLOCK * width,
            transcendentals=0,
        ),
        name="contract",
    )(cells, right, amplitude)


def ring(count, sign):
    return [(d, (d + sign) % count) for d in range(count)]


def ways(count):
    return [(sign, hops) for sign, hops in ((1, count // 2), (-1, (count - 1) // 2)) if hops]


def hop_sums(total_of, arrivals, hop, count):
    me = lax.axis_index("vb")
    sums = []
    for way, (sign, hops) in enumerate(ways(count)):
        if hop >= hops:
            sums.append(None)
            continue
        mine = total_of((me + sign * (hops - hop)) % count)
        if hop:
            mine = mine + arrivals[way].astype(jnp.float32)
        sums.append(mine.astype(jnp.bfloat16))
    return sums


def make_hop(sums, arrivals, count):
    made = []
    for way, (sign, _) in enumerate(ways(count)):
        going = sums[way]
        made.append(arrivals[way] if going is None else lax.ppermute(going, "vb", ring(count, sign)))
    return made


def shards(left_fit, right_fit, occ_energy, virt_energy, pair_list, domain_blocks):
    side = lax.axis_size("va")
    vb_count = lax.axis_size("vb")
    pair_count = lax.axis_size("pair")
    tile_rows = left_fit.shape[1]
    dom_blocks = domain_blocks.shape[1]
    va_index = lax.axis_index("va")
    vb_index = lax.axis_index("vb")
    pair_index = lax.axis_index("pair")
    energy_a = lax.dynamic_slice_in_dim(virt_energy, va_index * tile_rows, tile_rows)
    energy_b = lax.dynamic_slice_in_dim(virt_energy, vb_index * tile_rows, tile_rows)

    widths = [min(128, tile_rows)]
    while sum(widths) < tile_rows:
        widths.append(min(256, tile_rows - sum(widths)))
    parts = len(widths)
    spans = [slice(sum(widths[:part]), sum(widths[: part + 1])) for part in range(parts)]
    first_energy = pick_energy(occ_energy, pair_list[:, 0])
    second_energy = pick_energy(occ_energy, pair_list[:, 1])
    pair_energy = (first_energy + second_energy)[:, None, None]
    tiles = []
    for part in range(parts):
        columns = right_fit[:, spans[part]]
        tile = jnp.einsum("pak,pbk->pab", left_fit, columns, preferred_element_type=jnp.float32)
        tiles.append(tile.astype(jnp.bfloat16))
    turned = []
    for part in range(parts):
        rows = left_fit[:, spans[part]]
        tile = jnp.einsum("pbk,pak->pba", right_fit, rows, preferred_element_type=jnp.float32)
        turned.append(tile.astype(jnp.bfloat16))

    plane, column = [], []
    for part in range(parts):
        tile = tiles[part]
        if part:
            tile, plane[-1], turned[0] = lax.optimization_barrier((tile, plane[-1], turned[0]))
        plane.append(first_leg(tile, side))
    for part in range(parts):
        if part:
            plane[part], column[-1], turned[part] = lax.optimization_barrier(
                (plane[part], column[-1], turned[part])
            )
        column.append(next_leg(plane[part], "vb"))

    def amplitude_of(part):
        back = next_leg(column[part], "va")
        if part + 1 < parts:
            back, column[part + 1][:2] = lax.optimization_barrier((back, column[part + 1][:2]))
        mirrored = assemble(back)
        rows = spans[part]
        energy_gap = energy_a[None, None, rows] + energy_b[None, :, None] - pair_energy
        wide = 2.0 * turned[part].astype(jnp.float32) - mirrored.astype(jnp.float32)
        return (wide / energy_gap).astype(jnp.bfloat16)

    slab = AUX_BLK // (vb_count * pair_count)
    owner = domain_blocks // slab
    apart = (owner % pair_count - pair_index) % pair_count
    cells = ((apart * vb_count + owner // pair_count) * slab + domain_blocks % slab) * NOCC
    cells = (cells + pair_list[:, :1]).reshape(-1).astype(jnp.int32)

    send_type = jnp.bfloat16 if vb_count <= 4 else jnp.float32
    swap = [(c, (c + 1) % pair_count) for c in range(pair_count)]
    totals, hops = [], []
    for part in range(parts):
        keep, send = contract(cells, right_fit, amplitude_of(part), send_type)
        if part:
            send, hops[-1] = lax.optimization_barrier((send, hops[-1]))
            sums = hop_sums(totals[-1], hops[-1], 1, vb_count)
            send, sums = lax.optimization_barrier((send, sums))
            hops[-1] = make_hop(sums, hops[-1], vb_count)
        if part + 1 < parts:
            send, column[part + 1][2:] = lax.optimization_barrier((send, column[part + 1][2:]))
        got = lax.ppermute(send, "pair", swap)
        shape = (vb_count, slab * NOCC, BLOCK, widths[part])
        keep, got = keep.reshape(shape), got.reshape(shape)

        def total_of(owner, keep=keep, got=got):
            return pick(keep, owner) + pick(got, owner).astype(jnp.float32)

        totals.append(total_of)
        sums = hop_sums(total_of, None, 0, vb_count)
        if part:
            sums, hops[-1] = lax.optimization_barrier((sums, hops[-1]))
        if part + 1 < parts:
            sums, column[part + 1] = lax.optimization_barrier((sums, column[part + 1]))
        hops.append(make_hop(sums, None, vb_count))
    pieces = []
    for part in range(parts):
        arrived = hops[part]
        for hop in range(2 if part + 1 < parts else 1, vb_count // 2):
            arrived = make_hop(hop_sums(totals[part], arrived, hop, vb_count), arrived, vb_count)
        if part:
            arrived, pieces[-1] = lax.optimization_barrier((arrived, pieces[-1]))
        mine = totals[part](vb_index)
        for arrival in arrived:
            mine = mine + arrival.astype(jnp.float32)
        mine = mine.reshape(slab, NOCC, BLOCK, widths[part])
        pieces.append(mine.transpose(0, 2, 1, 3).reshape(slab * BLOCK, NOCC, widths[part]))
    return jnp.concatenate(pieces, axis=2)


def solution(mesh):
    return jax.shard_map(
        shards,
        mesh=mesh,
        in_specs=(
            P("pair", "va", None),
            P("pair", "vb", None),
            P(),
            P(),
            P("pair", None),
            P("pair", None),
        ),
        out_specs=P(("vb", "pair"), None, "va"),
        check_vma=False,
    )
```
